32 devices in a mesh: groups: 2 (over y), dp: 8 (over z, x), mp: 2 (over core).
Axes of the slice: x: 2, y: 2, z: 4, core: 2. Of those that a mesh axis runs over, the one named last changes fastest.
Arguments:
- inputs: bfloat16 [4096, 4096], P(('groups', 'dp'), 'mp'), parts along dimension 0, may hold values from -36 to 36
- output_gradient_rows: bfloat16 [4096, 14336], P(('groups', 'dp'), 'mp'), parts along dimension 0, may hold values from -144 to 144
- down_adapter_weight: bfloat16 [2, 64, 2048], P('mp', None, 'dp'), may hold values from -0.09375 to 0.09375
- up_adapter_weight: bfloat16 [2, 64, 7168], P('mp', None, 'dp'), may hold values from -0.046875 to 0.046875
- down_gradient_noise: float32 [2, 128, 2048], P('mp', 'groups', 'dp'), parts along dimension 1, may hold values from -5 to 5
- up_gradient_noise: float32 [2, 128, 7168], P('mp', 'groups', 'dp'), parts along dimension 1, may hold values from -5 to 5
Outputs:
- grad_a: float32 [2, 128, 2048], P('mp', 'groups', 'dp'), parts along dimension 1
- grad_b: float32 [2, 128, 7168], P('mp', 'groups', 'dp'), parts along dimension 1
The draws below stay inside these ranges and needn't reach their ends.
There are 2 independent parts, one for each index of `groups`. The reference program is written for one: setup_inputs(seed, part) draws one part's arguments, and reference() takes and returns one part's arrays. A program takes and returns all parts, laid end to end along the dimension named above; an argument that names none is the same for every part. Nothing has to cross between parts.
All inputs are finite; a program needn't handle non-finite values.
Results may differ from the reference program's by a relative error of at most 0.0003.
The reference program's roundings to bfloat16 on the way count: a program that leaves them out, or rounds other values in their place, can miss the bound.
Values may be sent and summed in bfloat16 or wider, within the bound.
A program may use at most 64 MiB of HBM per device.

```python
import math
import jax
import jax.numpy as jnp
from jax import lax

MODEL_WIDTH = 4096
UP_HIDDEN_UNITS = 14336
ADAPTER_RANK = 64
SEQ = 256
EXAMPLES = 8
TOKENS = 2048
N_MP = 2


def log_scales(key, count, low, high):
    return jnp.exp(jax.random.uniform(key, (count,), jnp.float32, math.log(low), math.log(high)))


def draw_inputs(key, part):
    key = jax.random.fold_in(key, 11)
    first, second, third = jax.random.split(key, 3)
    base = jax.random.truncated_normal(first, -4.0, 4.0, (TOKENS, MODEL_WIDTH), jnp.float32)
    rows = log_scales(second, TOKENS, 0.3, 3.0)
    cols = log_scales(third, MODEL_WIDTH, 0.3, 3.0)
    return (base * rows[:, None] * cols[None, :]).astype(jnp.bfloat16)


def draw_output_gradient_rows(key, part):
    key = jax.random.fold_in(key, 23)
    first, second, third, fourth = jax.random.split(key, 4)
    base = jax.random.truncated_normal(first, -4.0, 4.0, (TOKENS, UP_HIDDEN_UNITS), jnp.float32)
    cols = log_scales(third, UP_HIDDEN_UNITS, 0.3, 3.0)
    rows = log_scales(second, TOKENS, 0.3, 3.0)
    whole = jnp.repeat(log_scales(fourth, EXAMPLES, 0.25, 4.0), SEQ)
    return (base * (rows * whole)[:, None] * cols[None, :]).astype(jnp.bfloat16)


def level_of(key, shape, shards, low, largest):
    def one(dim, parts):
        steps = jax.random.uniform(jax.random.fold_in(jax.random.fold_in(key, 6), dim), (parts,), jnp.float32, low / len(shards), largest / len(shards))
        return jnp.repeat(jnp.exp(steps), shape[dim] // parts).reshape((-1,) + (1,) * (len(shape) - dim - 1))

    loudness = one(*shards[0])
    for cut in shards[1:]:
        loudness = loudness * one(*cut)
    return loudness


def noise(stream_key, dims, spread, reach, shards=(), held_as=jnp.bfloat16):
    entries = jax.random.normal(stream_key, dims, jnp.float32) * spread
    if len(shards) > 0:
        entries = level_of(stream_key, dims, shards, -0.22, 0.18) * entries
    return jnp.clip(entries, min=-reach, max=reach).astype(held_as)


def setup_inputs(seed: int = 0, part: int = 0) -> dict:
    keys = jax.random.split(jax.random.key(seed), 7)
    part_keys = jax.random.split(jax.random.fold_in(keys[6], part), 7)
    inputs = draw_inputs(jax.random.fold_in(jax.random.fold_in(keys[6], part), 71), part)
    output_gradient_rows = draw_output_gradient_rows(jax.random.fold_in(jax.random.fold_in(keys[6], part), 71), part)
    down_adapter_weight = noise(keys[2], (N_MP, ADAPTER_RANK, MODEL_WIDTH // N_MP), MODEL_WIDTH ** -0.5, 0.09375, ((0, 2), (2, 8)))
    up_adapter_weight = noise(keys[3], (N_MP, ADAPTER_RANK, UP_HIDDEN_UNITS // N_MP), UP_HIDDEN_UNITS ** -0.5, 0.046875, ((0, 2), (2, 8)))
    down_gradient_noise = noise(part_keys[4], (N_MP, ADAPTER_RANK, MODEL_WIDTH // N_MP), 1.0, 5.0, ((0, 2), (2, 8)), jnp.float32)
    up_gradient_noise = noise(part_keys[5], (N_MP, ADAPTER_RANK, UP_HIDDEN_UNITS // N_MP), 1.0, 5.0, ((0, 2), (2, 8)), jnp.float32)
    return dict(inputs=inputs, output_gradient_rows=output_gradient_rows, down_adapter_weight=down_adapter_weight, up_adapter_weight=up_adapter_weight, down_gradient_noise=down_gradient_noise, up_gradient_noise=up_gradient_noise)


def spread_shards(blocks):
    return jnp.transpose(blocks, (1, 0, 2)).reshape(blocks.shape[1], -1)

def fold_back(matrix):
    return jnp.transpose(matrix.reshape(matrix.shape[0], N_MP, -1), (1, 0, 2))

def reference(inputs, output_gradient_rows, down_adapter_weight, up_adapter_weight, down_gradient_noise, up_gradient_noise):
    clip_bound = 4.0 * (SEQ * ADAPTER_RANK * (MODEL_WIDTH + UP_HIDDEN_UNITS)) ** 0.5
    down_adapter_whole = spread_shards(down_adapter_weight)
    up_adapter_whole = spread_shards(up_adapter_weight)
    u_proj = lax.dot_general(inputs, down_adapter_whole, (((1,), (1,)), ((), ())), preferred_element_type=jnp.float32)
    v_proj = lax.dot_general(output_gradient_rows, up_adapter_whole, (((1,), (1,)), ((), ())), preferred_element_type=jnp.float32)
    u_low = u_proj.astype(jnp.bfloat16)
    v_low = v_proj.astype(jnp.bfloat16)

    def example_norm(index):
        start = index * SEQ
        x_rows = lax.dynamic_slice_in_dim(inputs, start, SEQ, 0)
        g_rows = lax.dynamic_slice_in_dim(output_gradient_rows, start, SEQ, 0)
        u_rows = lax.dynamic_slice_in_dim(u_low, start, SEQ, 0)
        v_rows = lax.dynamic_slice_in_dim(v_low, start, SEQ, 0)
        grad_x = jnp.dot(x_rows.T, v_rows, preferred_element_type=jnp.float32)
        grad_g = jnp.dot(u_rows.T, g_rows, preferred_element_type=jnp.float32)
        return jnp.sum(grad_x * grad_x) + jnp.sum(grad_g * grad_g)
    squares = lax.map(example_norm, jnp.arange(EXAMPLES, dtype=jnp.int32))
    clip_rate = clip_bound / jnp.maximum(jnp.sqrt(squares), clip_bound)
    token_rate = jnp.repeat(clip_rate, SEQ)
    scaled_u = (u_proj * token_rate[:, None]).astype(jnp.bfloat16)
    scaled_v = (v_proj * token_rate[:, None]).astype(jnp.bfloat16)
    sum_a = lax.dot_general(scaled_v, inputs, (((0,), (0,)), ((), ())), preferred_element_type=jnp.float32)
    sum_b = lax.dot_general(scaled_u, output_gradient_rows, (((0,), (0,)), ((), ())), preferred_element_type=jnp.float32)
    grad_a = (sum_a + 0.005 * clip_bound * spread_shards(down_gradient_noise)) / EXAMPLES
    grad_b = (sum_b + 0.005 * clip_bound * spread_shards(up_gradient_noise)) / EXAMPLES
    return (fold_back(grad_a), fold_back(grad_b))
```

```python
import functools
import math

import jax
import jax.numpy as jnp
from jax import lax
from jax.experimental import pallas as pl
from jax.experimental.pallas import tpu as pltpu
from jax.sharding import PartitionSpec as P

MODEL_WIDTH = 4096
UP_HIDDEN_UNITS = 14336
ADAPTER_RANK = 64
SEQ = 256

INNER = 2

clip_ratio = 4.0
noise_ratio = 0.005
clip_bound = clip_ratio * math.sqrt(SEQ * ADAPTER_RANK * (MODEL_WIDTH + UP_HIDDEN_UNITS))


def contract_last(left, right):
    return lax.dot_general(
        left, right, (((1,), (1,)), ((), ())), preferred_element_type=jnp.float32
    )


def contract_first(left, right):
    return lax.dot_general(
        left, right, (((0,), (0,)), ((), ())), preferred_element_type=jnp.float32
    )


def per_device(
    inputs,
    output_gradient_rows,
    down_adapter_weight,
    up_adapter_weight,
    down_gradient_noise,
    up_gradient_noise,
):
    a_half, b_half = (
        lax.all_gather(down_adapter_weight, "dp", axis=2, tiled=True),
        lax.all_gather(up_adapter_weight, "dp", axis=2, tiled=True),
    )
    u_part = contract_last(inputs, a_half[0])
    v_part = contract_last(output_gradient_rows, b_half[0])
    u_proj, v_proj = lax.psum((u_part, v_part), "mp")
    u_low = u_proj.astype(jnp.bfloat16)
    v_low = v_proj.astype(jnp.bfloat16)
    count = inputs.shape[0] // SEQ
    x_rows = inputs.reshape(count, SEQ, inputs.shape[1])
    g_rows = output_gradient_rows.reshape(count, SEQ, output_gradient_rows.shape[1])
    u_rows = u_low.reshape(count, SEQ, ADAPTER_RANK)
    v_rows = v_low.reshape(count, SEQ, ADAPTER_RANK)
    grad_x = jnp.einsum("esr,esd->erd", v_rows, x_rows, preferred_element_type=jnp.float32)
    grad_g = jnp.einsum("esr,esf->erf", u_rows, g_rows, preferred_element_type=jnp.float32)
    local_sq = jnp.sum(grad_x * grad_x, axis=(1, 2)) + jnp.sum(grad_g * grad_g, axis=(1, 2))
    squares = lax.psum(local_sq, "mp")
    clip_rate = clip_bound / jnp.maximum(jnp.sqrt(squares), clip_bound)
    token_rate = jnp.repeat(clip_rate, SEQ)
    scaled_u = (u_proj * token_rate[:, None]).astype(jnp.bfloat16)
    scaled_v = (v_proj * token_rate[:, None]).astype(jnp.bfloat16)
    part_a = contract_first(scaled_v, inputs)[None]
    part_b = contract_first(scaled_u, output_gradient_rows)[None]
    total_a, total_b = (
        lax.psum_scatter(part_a, "dp", scatter_dimension=2, tiled=True),
        lax.psum_scatter(part_b, "dp", scatter_dimension=2, tiled=True),
    )
    examples = count * lax.axis_size("dp")
    grad_a = (total_a + noise_ratio * clip_bound * down_gradient_noise) / examples
    grad_b = (total_b + noise_ratio * clip_bound * up_gradient_noise) / examples
    return (grad_a, grad_b)


def send(src, dst, send_sem, recv_sem, axis, index):
    copy = pltpu.make_async_remote_copy(
        src_ref=src,
        dst_ref=dst,
        send_sem=send_sem,
        recv_sem=recv_sem,
        device_id={axis: index},
        device_id_type=pl.DeviceIdType.MESH,
    )
    copy.start()
    return copy


def arrived(dst, send_sem, recv_sem, axis, index):
    pltpu.make_async_remote_copy(
        src_ref=dst,
        dst_ref=dst,
        send_sem=send_sem,
        recv_sem=recv_sem,
        device_id={axis: index},
        device_id_type=pl.DeviceIdType.MESH,
    ).wait_recv()


def target_order(depth):
    order = []
    for step in range((depth + 1) // 2):
        order.append(depth - 1 - step)
        if step != depth - 1 - step:
            order.append(step)
    return order


def kernel(
    depth,
    x_ref, g_ref, a_ref, b_ref, noise_a_ref, noise_b_ref,
    out_a_ref, out_b_ref,
    x_rows, g_rows, a_all, b_all, noise_a, noise_b,
    uv_mine, uv_other, sq_mine, sq_other,
    cross_out, cross_in, held, up_in, down_in,
    local_sem, gather_send, gather_recv, pair_send, pair_recv,
    cross_send, cross_recv, up_send, up_recv, down_send, down_recv,
):
    dp = lax.axis_index("dp")
    mp = lax.axis_index("mp")
    z = dp // INNER
    x = dp % INNER
    other_x = 1 - x
    across = z * INNER + other_x
    rank = a_ref.shape[1]
    wa = a_ref.shape[2]
    wb = b_ref.shape[2]
    examples = depth * INNER

    def local(src, dst, index):
        copy = pltpu.make_async_copy(src, dst, local_sem.at[index])
        copy.start()
        return copy

    own_a = local(a_ref.at[0], a_all.at[dp], 0)
    own_b = local(b_ref.at[0], b_all.at[dp], 1)
    load_x = local(x_ref, x_rows, 2)
    load_g = local(g_ref, g_rows, 3)
    load_na = local(noise_a_ref.at[0], noise_a, 4)
    load_nb = local(noise_b_ref.at[0], noise_b, 5)

    peers = [lax.rem(z + d, depth) for d in range(1, depth)]
    barrier = pltpu.get_barrier_semaphore()
    for axis, index in [("dp", across), ("mp", 1 - mp)] + [
        ("dp", p * INNER + x) for p in peers
    ]:
        pl.semaphore_signal(
            barrier, inc=1, device_id={axis: index}, device_id_type=pl.DeviceIdType.MESH
        )
    pl.semaphore_wait(barrier, 2 + len(peers))

    copies = []
    own_a.wait()
    own_b.wait()

    def give(slot, count, index):
        for which, whole in ((0, a_all), (1, b_all)):
            copies.append(
                send(
                    whole.at[slot], whole.at[slot],
                    gather_send.at[which, count], gather_recv.at[which, slot],
                    "dp", index,
                )
            )

    def take(slot):
        for which, whole in ((0, a_all), (1, b_all)):
            arrived(whole.at[slot], gather_send.at[which, 0], gather_recv.at[which, slot], "dp", across)

    give(dp, 0, across)
    for number, p in enumerate(peers):
        give(dp, 1 + number, p * INNER + x)

    def project(slot):
        u = contract_last(a_all[slot], x_rows[:, pl.ds(pl.multiple_of(slot * wa, 128), wa)])
        v = contract_last(b_all[slot], g_rows[:, pl.ds(pl.multiple_of(slot * wb, 128), wb)])
        return u, v

    load_x.wait()
    load_g.wait()
    u, v = project(dp)
    for number, p in enumerate(peers):
        slot = p * INNER + x
        take(slot)
        give(slot, depth + number, across)
        more = project(slot)
        u, v = u + more[0], v + more[1]
    for p in [z] + peers:
        slot = p * INNER + other_x
        take(slot)
        more = project(slot)
        u, v = u + more[0], v + more[1]

    uv_mine[0] = u
    uv_mine[1] = v
    copy = send(uv_mine, uv_other, pair_send.at[0], pair_recv.at[0], "mp", 1 - mp)
    copy.wait()
    u = u + uv_other[0]
    v = v + uv_other[1]
    u_low = u.astype(jnp.bfloat16)
    v_low = v.astype(jnp.bfloat16)

    def product(low, rows, block, width):
        return jnp.dot(
            low, rows[:, block * width:(block + 1) * width], preferred_element_type=jnp.float32
        )

    sq_a = jnp.zeros((1, wa), jnp.float32)
    sq_b = jnp.zeros((1, wb), jnp.float32)
    for block in range(examples):
        part = product(v_low, x_rows, block, wa)
        sq_a = sq_a + jnp.sum(part * part, axis=0, keepdims=True)
        part = product(u_low, g_rows, block, wb)
        sq_b = sq_b + jnp.sum(part * part, axis=0, keepdims=True)
    sq = jnp.sum(sq_a, axis=1, keepdims=True) + jnp.sum(sq_b, axis=1, keepdims=True)
    sq_mine[...] = jnp.broadcast_to(sq, sq_mine.shape)
    copy = send(sq_mine, sq_other, pair_send.at[1], pair_recv.at[1], "mp", 1 - mp)
    copy.wait()
    squares = sq_mine[...] + sq_other[...]
    rate = (clip_bound / jnp.maximum(jnp.sqrt(squares), clip_bound))[0:1, 0:1]
    u_scaled = (u * rate).astype(jnp.bfloat16)
    v_scaled = (v * rate).astype(jnp.bfloat16)

    def piece(target, side):
        slot = target * INNER + side
        part_a = jnp.dot(
            v_scaled, x_rows[:, pl.ds(pl.multiple_of(slot * wa, 128), wa)],
            preferred_element_type=jnp.float32,
        )
        part_b = jnp.dot(
            u_scaled, g_rows[:, pl.ds(pl.multiple_of(slot * wb, 128), wb)],
            preferred_element_type=jnp.float32,
        )
        return part_a, part_b

    order = target_order(depth)
    for target in order:
        part_a, part_b = piece(target, other_x)
        cross_out[target, :, :wa] = part_a
        cross_out[target, :, wa:] = part_b
        copies.append(
            send(
                cross_out.at[target], cross_in.at[target],
                cross_send.at[target], cross_recv.at[target], "dp", across,
            )
        )
    for target in order:
        part_a, part_b = piece(target, x)
        held[target, :, :wa] = part_a
        held[target, :, wa:] = part_b

    above = dp + INNER
    below = dp - INNER

    def from_below(target):
        arrived(up_in.at[target], up_send.at[target], up_recv.at[target], "dp", dp)
        held[target] = held[target] + up_in[target]

    def from_above(target):
        arrived(down_in.at[target], down_send.at[target], down_recv.at[target], "dp", dp)
        held[target] = held[target] + down_in[target]

    for target in order:
        arrived(cross_in.at[target], cross_send.at[target], cross_recv.at[target], "dp", across)
        held[target] = held[target] + cross_in[target]

        @pl.when(z < target)
        def _():
            @pl.when(z > 0)
            def _():
                from_below(target)

            send(held.at[target], up_in.at[target], up_send.at[target], up_recv.at[target], "dp", above)

        @pl.when(z > target)
        def _():
            @pl.when(z < depth - 1)
            def _():
                from_above(target)

            send(
                held.at[target], down_in.at[target],
                down_send.at[target], down_recv.at[target], "dp", below,
            )

    load_na.wait()
    load_nb.wait()
    scale = noise_ratio * clip_bound
    for target in range(depth):

        @pl.when(z == target)
        def _():
            if target > 0:
                from_below(target)
            if target < depth - 1:
                from_above(target)
            out_a_ref[0] = (held[target, :, :wa] + scale * noise_a[...]) / examples
            out_b_ref[0] = (held[target, :, wa:] + scale * noise_b[...]) / examples

    for copy in copies:
        copy.wait_send()
    for target in range(depth):

        @pl.when(z < target)
        def _():
            pltpu.make_async_remote_copy(
                src_ref=held.at[target], dst_ref=up_in.at[target],
                send_sem=up_send.at[target], recv_sem=up_recv.at[target],
                device_id={"dp": above}, device_id_type=pl.DeviceIdType.MESH,
            ).wait_send()

        @pl.when(z > target)
        def _():
            pltpu.make_async_remote_copy(
                src_ref=held.at[target], dst_ref=down_in.at[target],
                send_sem=down_send.at[target], recv_sem=down_recv.at[target],
                device_id={"dp": below}, device_id_type=pl.DeviceIdType.MESH,
            ).wait_send()


def fused(depth, inputs, rows, down, up, noise_a, noise_b):
    rank, wa = down.shape[1:]
    wb = up.shape[2]
    dp = depth * INNER
    f32, bf16 = jnp.float32, jnp.bfloat16
    dma = pltpu.SemaphoreType.DMA
    return pl.pallas_call(
        functools.partial(kernel, depth),
        out_shape=(
            jax.ShapeDtypeStruct(noise_a.shape, f32),
            jax.ShapeDtypeStruct(noise_b.shape, f32),
        ),
        in_specs=[pl.BlockSpec(memory_space=pl.ANY)] * 6,
        out_specs=(pl.BlockSpec(memory_space=pltpu.VMEM), pl.BlockSpec(memory_space=pltpu.VMEM)),
        scratch_shapes=[
            pltpu.VMEM(inputs.shape, bf16),
            pltpu.VMEM(rows.shape, bf16),
            pltpu.VMEM((dp, rank, wa), bf16),
            pltpu.VMEM((dp, rank, wb), bf16),
            pltpu.VMEM((rank, wa), f32),
            pltpu.VMEM((rank, wb), f32),
            pltpu.VMEM((2, rank, SEQ), f32),
            pltpu.VMEM((2, rank, SEQ), f32),
            pltpu.VMEM((8, 128), f32),
            pltpu.VMEM((8, 128), f32),
            pltpu.VMEM((depth, rank, wa + wb), f32),
            pltpu.VMEM((depth, rank, wa + wb), f32),
            pltpu.VMEM((depth, rank, wa + wb), f32),
            pltpu.VMEM((depth, rank, wa + wb), f32),
            pltpu.VMEM((depth, rank, wa + wb), f32),
            dma((6,)),
            dma((2, 2 * depth)),
            dma((2, dp)),
            dma((2,)),
            dma((2,)),
            dma((depth,)),
            dma((depth,)),
            dma((depth,)),
            dma((depth,)),
            dma((depth,)),
            dma((depth,)),
        ],
        compiler_params=pltpu.CompilerParams(
            collective_id=0, has_side_effects=True, vmem_limit_bytes=40 * 1024 * 1024
        ),
        cost_estimate=pl.CostEstimate(
            flops=6 * rank * SEQ * dp * (wa + wb),
            bytes_accessed=2 * SEQ * dp * (wa + wb),
            transcendentals=0,
        ),
    )(inputs, rows, down, up, noise_a, noise_b)


def solution(mesh):
    in_specs = (
        P(("groups", "dp"), "mp"),
        P(("groups", "dp"), "mp"),
        P("mp", None, "dp"),
        P("mp", None, "dp"),
        P("mp", "groups", "dp"),
        P("mp", "groups", "dp"),
    )
    out_specs = (P("mp", "groups", "dp"), P("mp", "groups", "dp"))
    devices = mesh.shape["dp"]

    def body(inputs, rows, down, up, noise_a, noise_b):
        fits = (
            devices % INNER == 0
            and 4 <= devices <= 16
            and mesh.shape["mp"] == 2
            and inputs.shape[0] == SEQ
            and down.shape[2] % 128 == 0
            and up.shape[2] % 128 == 0
        )
        if fits:
            return fused(devices // INNER, inputs, rows, down, up, noise_a, noise_b)
        return per_device(inputs, rows, down, up, noise_a, noise_b)

    return jax.shard_map(
        body, mesh=mesh, in_specs=in_specs, out_specs=out_specs, check_vma=False
    )
```

```python
import functools
import math

import jax
import jax.numpy as jnp
from jax import lax
from jax.experimental import pallas as pl
from jax.experimental.pallas import tpu as pltpu
from jax.sharding import PartitionSpec as P

MODEL_WIDTH = 4096
UP_HIDDEN_UNITS = 14336
ADAPTER_RANK = 64
SEQ = 256

INNER = 2
GATHER_CUTS = 2
REDUCE_CUTS = 2

clip_ratio = 4.0
noise_ratio = 0.005
clip_bound = clip_ratio * math.sqrt(SEQ * ADAPTER_RANK * (MODEL_WIDTH + UP_HIDDEN_UNITS))


def contract_last(left, right):
    return lax.dot_general(
        left, right, (((1,), (1,)), ((), ())), preferred_element_type=jnp.float32
    )


def contract_first(left, right):
    return lax.dot_general(
        left, right, (((0,), (0,)), ((), ())), preferred_element_type=jnp.float32
    )


def per_device(
    inputs,
    output_gradient_rows,
    down_adapter_weight,
    up_adapter_weight,
    down_gradient_noise,
    up_gradient_noise,
):
    a_half, b_half = (
        lax.all_gather(down_adapter_weight, "dp", axis=2, tiled=True),
        lax.all_gather(up_adapter_weight, "dp", axis=2, tiled=True),
    )
    u_part = contract_last(inputs, a_half[0])
    v_part = contract_last(output_gradient_rows, b_half[0])
    u_proj, v_proj = lax.psum((u_part, v_part), "mp")
    u_low = u_proj.astype(jnp.bfloat16)
    v_low = v_proj.astype(jnp.bfloat16)
    count = inputs.shape[0] // SEQ
    x_rows = inputs.reshape(count, SEQ, inputs.shape[1])
    g_rows = output_gradient_rows.reshape(count, SEQ, output_gradient_rows.shape[1])
    u_rows = u_low.reshape(count, SEQ, ADAPTER_RANK)
    v_rows = v_low.reshape(count, SEQ, ADAPTER_RANK)
    grad_x = jnp.einsum("esr,esd->erd", v_rows, x_rows, preferred_element_type=jnp.float32)
    grad_g = jnp.einsum("esr,esf->erf", u_rows, g_rows, preferred_element_type=jnp.float32)
    local_sq = jnp.sum(grad_x * grad_x, axis=(1, 2)) + jnp.sum(grad_g * grad_g, axis=(1, 2))
    squares = lax.psum(local_sq, "mp")
    clip_rate = clip_bound / jnp.maximum(jnp.sqrt(squares), clip_bound)
    token_rate = jnp.repeat(clip_rate, SEQ)
    scaled_u = (u_proj * token_rate[:, None]).astype(jnp.bfloat16)
    scaled_v = (v_proj * token_rate[:, None]).astype(jnp.bfloat16)
    part_a = contract_first(scaled_v, inputs)[None]
    part_b = contract_first(scaled_u, output_gradient_rows)[None]
    total_a, total_b = (
        lax.psum_scatter(part_a, "dp", scatter_dimension=2, tiled=True),
        lax.psum_scatter(part_b, "dp", scatter_dimension=2, tiled=True),
    )
    examples = count * lax.axis_size("dp")
    grad_a = (total_a + noise_ratio * clip_bound * down_gradient_noise) / examples
    grad_b = (total_b + noise_ratio * clip_bound * up_gradient_noise) / examples
    return (grad_a, grad_b)


def remote(src, dst, send_sem, recv_sem, axis, index):
    return pltpu.make_async_remote_copy(
        src_ref=src,
        dst_ref=dst,
        send_sem=send_sem,
        recv_sem=recv_sem,
        device_id={axis: index},
        device_id_type=pl.DeviceIdType.MESH,
    )


def gather_order(depth):
    return [sorted((p for p in range(depth) if p != z), key=lambda p: abs(p - z)) for z in range(depth)]


def reduce_order(depth):
    table = []
    for z in range(depth):
        up = list(range(depth - 1, z, -1))
        down = list(range(z))
        table.append((up + down if len(up) >= len(down) else down + up) + [z])
    return table


def pick(table, step, z):
    entry = jnp.int32(table[0][step])
    for row in range(1, len(table)):
        entry = jnp.where(z == row, jnp.int32(table[row][step]), entry)
    return entry


def kernel(
    depth,
    x_ref, g_ref, a_ref, b_ref, noise_a_ref, noise_b_ref,
    out_a_ref, out_b_ref,
    x_rows, g_rows, a_all, b_all, noise_a, noise_b,
    uv_mine, uv_other, sq_mine, sq_other,
    cross_out, cross_in, held, up_in, down_in,
    local_sem, gather_send, gather_recv, pair_send, pair_recv,
    cross_send, cross_recv, up_send, up_recv, down_send, down_recv,
):
    dp = lax.axis_index("dp")
    mp = lax.axis_index("mp")
    z = dp // INNER
    x = dp % INNER
    other_x = 1 - x
    across = z * INNER + other_x
    above = dp + INNER
    below = dp - INNER
    rank = a_ref.shape[1]
    wa = a_ref.shape[2]
    wb = b_ref.shape[2]
    examples = depth * INNER
    has_above = z < depth - 1
    has_below = z > 0

    def local(src, dst, index):
        copy = pltpu.make_async_copy(src, dst, local_sem.at[index])
        copy.start()
        return copy

    own_a = local(a_ref.at[0], a_all.at[dp], 0)
    own_b = local(b_ref.at[0], b_all.at[dp], 1)
    load_x = local(x_ref, x_rows, 2)
    load_g = local(g_ref, g_rows, 3)
    load_na = local(noise_a_ref.at[0], noise_a, 4)
    load_nb = local(noise_b_ref.at[0], noise_b, 5)

    barrier = pltpu.get_barrier_semaphore()

    def greet(axis, index):
        pl.semaphore_signal(
            barrier, inc=1, device_id={axis: index}, device_id_type=pl.DeviceIdType.MESH
        )

    greet("dp", across)
    greet("mp", 1 - mp)

    @pl.when(has_above)
    def _():
        greet("dp", above)

    @pl.when(has_below)
    def _():
        greet("dp", below)

    @pl.when(has_above & has_below)
    def _():
        pl.semaphore_wait(barrier, 4)

    @pl.when(jnp.logical_not(has_above & has_below))
    def _():
        pl.semaphore_wait(barrier, 3)

    own_a.wait()
    own_b.wait()

    def chunk(which, cut):
        size = rank // GATHER_CUTS
        return ((a_all, b_all)[which]), pl.ds(cut * size, size)

    parts = [(which, cut) for cut in range(GATHER_CUTS) for which in (0, 1)]

    def give(part, row, way, index):
        which, cut = part
        whole, rows = chunk(which, cut)
        slot = row * INNER + x
        return remote(
            whole.at[slot, rows], whole.at[slot, rows],
            gather_send.at[way, which, cut, row], gather_recv.at[which, cut, slot],
            "dp", index,
        )

    def take(part, slot):
        which, cut = part
        whole, rows = chunk(which, cut)
        remote(
            whole.at[slot, rows], whole.at[slot, rows],
            gather_send.at[0, which, cut, 0], gather_recv.at[which, cut, slot],
            "dp", across,
        ).wait_recv()

    def pass_on(part, row, act):
        @pl.when(has_above & (row <= z))
        def _():
            act(give(part, row, 1, above))

        @pl.when(has_below & (row >= z))
        def _():
            act(give(part, row, 2, below))

        act(give(part, row, 0, across))

    def start(copy):
        copy.start()

    def finish(copy):
        copy.wait_send()

    def project(slot):
        u = contract_last(a_all[slot], x_rows[:, pl.ds(pl.multiple_of(slot * wa, 128), wa)])
        v = contract_last(b_all[slot], g_rows[:, pl.ds(pl.multiple_of(slot * wb, 128), wb)])
        return u, v

    for part in parts:
        pass_on(part, z, start)
    near = gather_order(depth)
    rows_of = [pick(near, step, z) for step in range(depth - 1)]
    load_x.wait()
    load_g.wait()
    u, v = project(dp)

    def take_across(row, u, v):
        slot = row * INNER + other_x
        for part in parts:
            take(part, slot)
        more = project(slot)
        return u + more[0], v + more[1]

    last = z
    for row in rows_of:
        for part in parts:
            take(part, row * INNER + x)
            pass_on(part, row, start)
        more = project(row * INNER + x)
        u, v = u + more[0], v + more[1]
        u, v = take_across(last, u, v)
        last = row
    u, v = take_across(last, u, v)

    uv_mine[0] = u
    uv_mine[1] = v
    copy = remote(uv_mine, uv_other, pair_send.at[0], pair_recv.at[0], "mp", 1 - mp)
    copy.start()
    copy.wait()
    u = u + uv_other[0]
    v = v + uv_other[1]
    u_low = u.astype(jnp.bfloat16)
    v_low = v.astype(jnp.bfloat16)

    def product(low, rows, block, width):
        return jnp.dot(
            low, rows[:, block * width:(block + 1) * width], preferred_element_type=jnp.float32
        )

    sq_a = jnp.zeros((1, wa), jnp.float32)
    sq_b = jnp.zeros((1, wb), jnp.float32)
    for block in range(examples):
        part = product(v_low, x_rows, block, wa)
        sq_a = sq_a + jnp.sum(part * part, axis=0, keepdims=True)
        part = product(u_low, g_rows, block, wb)
        sq_b = sq_b + jnp.sum(part * part, axis=0, keepdims=True)
    sq = jnp.sum(sq_a, axis=1, keepdims=True) + jnp.sum(sq_b, axis=1, keepdims=True)
    sq_mine[...] = jnp.broadcast_to(sq, sq_mine.shape)
    copy = remote(sq_mine, sq_other, pair_send.at[1], pair_recv.at[1], "mp", 1 - mp)
    copy.start()
    copy.wait()
    squares = sq_mine[...] + sq_other[...]
    rate = (clip_bound / jnp.maximum(jnp.sqrt(squares), clip_bound))[0:1, 0:1]
    u_scaled = (u * rate).astype(jnp.bfloat16)
    v_scaled = (v * rate).astype(jnp.bfloat16)

    def piece(target, side):
        slot = target * INNER + side
        part_a = jnp.dot(
            v_scaled, x_rows[:, pl.ds(pl.multiple_of(slot * wa, 128), wa)],
            preferred_element_type=jnp.float32,
        )
        part_b = jnp.dot(
            u_scaled, g_rows[:, pl.ds(pl.multiple_of(slot * wb, 128), wb)],
            preferred_element_type=jnp.float32,
        )
        return part_a, part_b

    far = reduce_order(depth)
    targets = [pick(far, step, z) for step in range(depth)]

    def sums(src, dst, send_sem, recv_sem, target, cut, index):
        size = rank // REDUCE_CUTS
        rows = pl.ds(cut * size, size)
        return remote(
            src.at[target, rows], dst.at[target, rows],
            send_sem.at[target, cut], recv_sem.at[target, cut], "dp", index,
        )

    def over(target, cut):
        return sums(cross_out, cross_in, cross_send, cross_recv, target, cut, across)

    def upward(target, cut):
        return sums(held, up_in, up_send, up_recv, target, cut, above)

    def downward(target, cut):
        return sums(held, down_in, down_send, down_recv, target, cut, below)

    def add(target, cut, arriving):
        size = rank // REDUCE_CUTS
        rows = pl.ds(cut * size, size)
        held[target, rows] = held[target, rows] + arriving[target, rows]

    for target in targets:
        part_a, part_b = piece(target, other_x)
        cross_out[target, :, :wa] = part_a
        cross_out[target, :, wa:] = part_b
        for cut in range(REDUCE_CUTS):
            over(target, cut).start()
    for target in targets:
        part_a, part_b = piece(target, x)
        held[target, :, :wa] = part_a
        held[target, :, wa:] = part_b

    for target in targets[:-1]:
        for cut in range(REDUCE_CUTS):
            over(target, cut).wait_recv()
            add(target, cut, cross_in)

            @pl.when(z < target)
            def _():
                @pl.when(has_below)
                def _():
                    upward(target, cut).wait_recv()
                    add(target, cut, up_in)

                upward(target, cut).start()

            @pl.when(z > target)
            def _():
                @pl.when(has_above)
                def _():
                    downward(target, cut).wait_recv()
                    add(target, cut, down_in)

                downward(target, cut).start()

    load_na.wait()
    load_nb.wait()
    scale = noise_ratio * clip_bound
    for cut in range(REDUCE_CUTS):
        over(z, cut).wait_recv()
        add(z, cut, cross_in)

        @pl.when(has_below)
        def _():
            upward(z, cut).wait_recv()
            add(z, cut, up_in)

        @pl.when(has_above)
        def _():
            downward(z, cut).wait_recv()
            add(z, cut, down_in)

    out_a_ref[0] = (held[z, :, :wa] + scale * noise_a[...]) / examples
    out_b_ref[0] = (held[z, :, wa:] + scale * noise_b[...]) / examples

    for row in [z] + rows_of:
        for part in parts:
            pass_on(part, row, finish)
    for target in targets:
        for cut in range(REDUCE_CUTS):
            over(target, cut).wait_send()

            @pl.when(z < target)
            def _():
                upward(target, cut).wait_send()

            @pl.when(z > target)
            def _():
                downward(target, cut).wait_send()


def fused(depth, inputs, rows, down, up, noise_a, noise_b):
    rank, wa = down.shape[1:]
    wb = up.shape[2]
    dp = depth * INNER
    f32, bf16 = jnp.float32, jnp.bfloat16
    dma = pltpu.SemaphoreType.DMA
    return pl.pallas_call(
        functools.partial(kernel, depth),
        out_shape=(
            jax.ShapeDtypeStruct(noise_a.shape, f32),
            jax.ShapeDtypeStruct(noise_b.shape, f32),
        ),
        in_specs=[pl.BlockSpec(memory_space=pltpu.HBM)] * 6,
        out_specs=(pl.BlockSpec(memory_space=pltpu.VMEM), pl.BlockSpec(memory_space=pltpu.VMEM)),
        scratch_shapes=[
            pltpu.VMEM(inputs.shape, bf16),
            pltpu.VMEM(rows.shape, bf16),
            pltpu.VMEM((dp, rank, wa), bf16),
            pltpu.VMEM((dp, rank, wb), bf16),
            pltpu.VMEM((rank, wa), f32),
            pltpu.VMEM((rank, wb), f32),
            pltpu.VMEM((2, rank, SEQ), f32),
            pltpu.VMEM((2, rank, SEQ), f32),
            pltpu.VMEM((8, 128), f32),
            pltpu.VMEM((8, 128), f32),
            pltpu.VMEM((depth, rank, wa + wb), f32),
            pltpu.VMEM((depth, rank, wa + wb), f32),
            pltpu.VMEM((depth, rank, wa + wb), f32),
            pltpu.VMEM((depth, rank, wa + wb), f32),
            pltpu.VMEM((depth, rank, wa + wb), f32),
            dma((6,)),
            dma((3, 2, GATHER_CUTS, depth)),
            dma((2, GATHER_CUTS, dp)),
            dma((2,)),
            dma((2,)),
            dma((depth, REDUCE_CUTS)),
            dma((depth, REDUCE_CUTS)),
            dma((depth, REDUCE_CUTS)),
            dma((depth, REDUCE_CUTS)),
            dma((depth, REDUCE_CUTS)),
            dma((depth, REDUCE_CUTS)),
        ],
        compiler_params=pltpu.CompilerParams(
            collective_id=0, has_side_effects=True, vmem_limit_bytes=40 * 1024 * 1024
        ),
        cost_estimate=pl.CostEstimate(
            flops=6 * rank * SEQ * dp * (wa + wb),
            bytes_accessed=2 * SEQ * dp * (wa + wb),
            transcendentals=0,
        ),
    )(inputs, rows, down, up, noise_a, noise_b)


def solution(mesh):
    in_specs = (
        P(("groups", "dp"), "mp"),
        P(("groups", "dp"), "mp"),
        P("mp", None, "dp"),
        P("mp", None, "dp"),
        P("mp", "groups", "dp"),
        P("mp", "groups", "dp"),
    )
    out_specs = (P("mp", "groups", "dp"), P("mp", "groups", "dp"))
    devices = mesh.shape["dp"]

    def body(inputs, rows, down, up, noise_a, noise_b):
        fits = (
            devices % INNER == 0
            and 4 <= devices <= 16
            and mesh.shape["mp"] == 2
            and inputs.shape[0] == SEQ
            and down.shape[2] % 128 == 0
            and up.shape[2] % 128 == 0
        )
        if fits:
            return fused(devices // INNER, inputs, rows, down, up, noise_a, noise_b)
        return per_device(inputs, rows, down, up, noise_a, noise_b)

    return jax.shard_map(
        body, mesh=mesh, in_specs=in_specs, out_specs=out_specs, check_vma=False
    )
```

```python
import functools
import math

import jax
import jax.numpy as jnp
from jax import lax
from jax.experimental import pallas as pl
from jax.experimental.pallas import tpu as pltpu
from jax.sharding import PartitionSpec as P

MODEL_WIDTH = 4096
UP_HIDDEN_UNITS = 14336
ADAPTER_RANK = 64
SEQ = 256

INNER = 2
GATHER_CUTS = 2
REDUCE_CUTS = 2

clip_ratio = 4.0
noise_ratio = 0.005
clip_bound = clip_ratio * math.sqrt(SEQ * ADAPTER_RANK * (MODEL_WIDTH + UP_HIDDEN_UNITS))


def contract_last(left, right):
    return lax.dot_general(
        left, right, (((1,), (1,)), ((), ())), preferred_element_type=jnp.float32
    )


def contract_first(left, right):
    return lax.dot_general(
        left, right, (((0,), (0,)), ((), ())), preferred_element_type=jnp.float32
    )


def per_device(
    inputs,
    output_gradient_rows,
    down_adapter_weight,
    up_adapter_weight,
    down_gradient_noise,
    up_gradient_noise,
):
    a_half, b_half = (
        lax.all_gather(down_adapter_weight, "dp", axis=2, tiled=True),
        lax.all_gather(up_adapter_weight, "dp", axis=2, tiled=True),
    )
    u_part = contract_last(inputs, a_half[0])
    v_part = contract_last(output_gradient_rows, b_half[0])
    u_proj, v_proj = lax.psum((u_part, v_part), "mp")
    u_low = u_proj.astype(jnp.bfloat16)
    v_low = v_proj.astype(jnp.bfloat16)
    count = inputs.shape[0] // SEQ
    x_rows = inputs.reshape(count, SEQ, inputs.shape[1])
    g_rows = output_gradient_rows.reshape(count, SEQ, output_gradient_rows.shape[1])
    u_rows = u_low.reshape(count, SEQ, ADAPTER_RANK)
    v_rows = v_low.reshape(count, SEQ, ADAPTER_RANK)
    grad_x = jnp.einsum("esr,esd->erd", v_rows, x_rows, preferred_element_type=jnp.float32)
    grad_g = jnp.einsum("esr,esf->erf", u_rows, g_rows, preferred_element_type=jnp.float32)
    local_sq = jnp.sum(grad_x * grad_x, axis=(1, 2)) + jnp.sum(grad_g * grad_g, axis=(1, 2))
    squares = lax.psum(local_sq, "mp")
    clip_rate = clip_bound / jnp.maximum(jnp.sqrt(squares), clip_bound)
    token_rate = jnp.repeat(clip_rate, SEQ)
    scaled_u = (u_proj * token_rate[:, None]).astype(jnp.bfloat16)
    scaled_v = (v_proj * token_rate[:, None]).astype(jnp.bfloat16)
    part_a = contract_first(scaled_v, inputs)[None]
    part_b = contract_first(scaled_u, output_gradient_rows)[None]
    total_a, total_b = (
        lax.psum_scatter(part_a, "dp", scatter_dimension=2, tiled=True),
        lax.psum_scatter(part_b, "dp", scatter_dimension=2, tiled=True),
    )
    examples = count * lax.axis_size("dp")
    grad_a = (total_a + noise_ratio * clip_bound * down_gradient_noise) / examples
    grad_b = (total_b + noise_ratio * clip_bound * up_gradient_noise) / examples
    return (grad_a, grad_b)


def remote(src, dst, send_sem, recv_sem, axis, index):
    return pltpu.make_async_remote_copy(
        src_ref=src,
        dst_ref=dst,
        send_sem=send_sem,
        recv_sem=recv_sem,
        device_id={axis: index},
        device_id_type=pl.DeviceIdType.MESH,
    )


def gather_order(depth):
    return [sorted((p for p in range(depth) if p != z), key=lambda p: abs(p - z)) for z in range(depth)]


def reduce_order(depth):
    table = []
    for z in range(depth):
        up = list(range(depth - 1, z, -1))
        down = list(range(z))
        table.append((up + down if len(up) >= len(down) else down + up) + [z])
    return table


def pick(table, step, z):
    entry = jnp.int32(table[0][step])
    for row in range(1, len(table)):
        entry = jnp.where(z == row, jnp.int32(table[row][step]), entry)
    return entry


def kernel(
    depth,
    x_ref, g_ref, a_ref, b_ref, noise_a_ref, noise_b_ref,
    out_a_ref, out_b_ref,
    x_rows, g_rows, a_all, b_all, noise_a, noise_b,
    uv_mine, uv_other, sq_mine, sq_other,
    cross_out, cross_in, held, up_in, down_in,
    local_sem, gather_send, gather_recv, pair_send, pair_recv,
    cross_send, cross_recv, up_send, up_recv, down_send, down_recv,
):
    dp = lax.axis_index("dp")
    mp = lax.axis_index("mp")
    z = dp // INNER
    x = dp % INNER
    other_x = 1 - x
    across = z * INNER + other_x
    above = dp + INNER
    below = dp - INNER
    rank = a_ref.shape[1]
    wa = a_ref.shape[2]
    wb = b_ref.shape[2]
    examples = depth * INNER
    has_above = z < depth - 1
    has_below = z > 0

    def local(src, dst, index):
        copy = pltpu.make_async_copy(src, dst, local_sem.at[index])
        copy.start()
        return copy

    own_a = local(a_ref.at[0], a_all.at[dp], 0)
    own_b = local(b_ref.at[0], b_all.at[dp], 1)
    load_x = local(x_ref, x_rows, 2)
    load_g = local(g_ref, g_rows, 3)
    load_na = local(noise_a_ref.at[0], noise_a, 4)
    load_nb = local(noise_b_ref.at[0], noise_b, 5)

    barrier = pltpu.get_barrier_semaphore()

    def greet(axis, index):
        pl.semaphore_signal(
            barrier, inc=1, device_id={axis: index}, device_id_type=pl.DeviceIdType.MESH
        )

    greet("dp", across)
    greet("mp", 1 - mp)

    @pl.when(has_above)
    def _():
        greet("dp", above)

    @pl.when(has_below)
    def _():
        greet("dp", below)

    @pl.when(has_above & has_below)
    def _():
        pl.semaphore_wait(barrier, 4)

    @pl.when(jnp.logical_not(has_above & has_below))
    def _():
        pl.semaphore_wait(barrier, 3)

    own_a.wait()
    own_b.wait()

    def chunk(which, cut):
        size = rank // GATHER_CUTS
        return ((a_all, b_all)[which]), pl.ds(cut * size, size)

    parts = [(which, cut) for cut in range(GATHER_CUTS) for which in (0, 1)]

    def give(part, row, way, index):
        which, cut = part
        whole, rows = chunk(which, cut)
        slot = row * INNER + x
        return remote(
            whole.at[slot, rows], whole.at[slot, rows],
            gather_send.at[way, which, cut, row], gather_recv.at[which, cut, slot],
            "dp", index,
        )

    def take(part, slot):
        which, cut = part
        whole, rows = chunk(which, cut)
        remote(
            whole.at[slot, rows], whole.at[slot, rows],
            gather_send.at[0, which, cut, 0], gather_recv.at[which, cut, slot],
            "dp", across,
        ).wait_recv()

    def pass_on(part, row, act):
        @pl.when(has_above & (row <= z))
        def _():
            act(give(part, row, 1, above))

        @pl.when(has_below & (row >= z))
        def _():
            act(give(part, row, 2, below))

        act(give(part, row, 0, across))

    def start(copy):
        copy.start()

    def finish(copy):
        copy.wait_send()

    def project(slot):
        u = contract_last(a_all[slot], x_rows[:, pl.ds(pl.multiple_of(slot * wa, 128), wa)])
        v = contract_last(b_all[slot], g_rows[:, pl.ds(pl.multiple_of(slot * wb, 128), wb)])
        return u, v

    for part in parts:
        pass_on(part, z, start)
    near = gather_order(depth)
    rows_of = [pick(near, step, z) for step in range(depth - 1)]
    load_x.wait()
    load_g.wait()
    u, v = project(dp)

    def take_across(row, u, v):
        slot = row * INNER + other_x
        for part in parts:
            take(part, slot)
        more = project(slot)
        return u + more[0], v + more[1]

    last = z
    for row in rows_of:
        for part in parts:
            take(part, row * INNER + x)
            pass_on(part, row, start)
        more = project(row * INNER + x)
        u, v = u + more[0], v + more[1]
        u, v = take_across(last, u, v)
        last = row
    u, v = take_across(last, u, v)

    uv_mine[0] = u
    uv_mine[1] = v
    copy = remote(uv_mine, uv_other, pair_send.at[0], pair_recv.at[0], "mp", 1 - mp)
    copy.start()
    copy.wait()
    u = u + uv_other[0]
    v = v + uv_other[1]
    u_low = u.astype(jnp.bfloat16)
    v_low = v.astype(jnp.bfloat16)

    def product(low, rows, block, width):
        return jnp.dot(
            low, rows[:, block * width:(block + 1) * width], preferred_element_type=jnp.float32
        )

    sq_a = jnp.zeros((1, wa), jnp.float32)
    sq_b = jnp.zeros((1, wb), jnp.float32)
    for block in range(examples):
        part = product(v_low, x_rows, block, wa)
        sq_a = sq_a + jnp.sum(part * part, axis=0, keepdims=True)
        part = product(u_low, g_rows, block, wb)
        sq_b = sq_b + jnp.sum(part * part, axis=0, keepdims=True)
    sq = jnp.sum(sq_a, axis=1, keepdims=True) + jnp.sum(sq_b, axis=1, keepdims=True)
    sq_mine[...] = jnp.broadcast_to(sq, sq_mine.shape)
    copy = remote(sq_mine, sq_other, pair_send.at[1], pair_recv.at[1], "mp", 1 - mp)
    copy.start()
    copy.wait()
    squares = sq_mine[...] + sq_other[...]
    rate = (clip_bound / jnp.maximum(jnp.sqrt(squares), clip_bound))[0:1, 0:1]
    u_scaled = (u * rate).astype(jnp.bfloat16)
    v_scaled = (v * rate).astype(jnp.bfloat16)

    def piece(target, side):
        slot = target * INNER + side
        part_a = jnp.dot(
            v_scaled, x_rows[:, pl.ds(pl.multiple_of(slot * wa, 128), wa)],
            preferred_element_type=jnp.float32,
        )
        part_b = jnp.dot(
            u_scaled, g_rows[:, pl.ds(pl.multiple_of(slot * wb, 128), wb)],
            preferred_element_type=jnp.float32,
        )
        return part_a, part_b

    far = reduce_order(depth)
    targets = [pick(far, step, z) for step in range(depth)]

    def sums(src, dst, send_sem, recv_sem, target, cut, index):
        size = rank // REDUCE_CUTS
        rows = pl.ds(cut * size, size)
        return remote(
            src.at[target, rows], dst.at[target, rows],
            send_sem.at[target, cut], recv_sem.at[target, cut], "dp", index,
        )

    def over(target, cut):
        return sums(cross_out, cross_in, cross_send, cross_recv, target, cut, across)

    def upward(target, cut):
        return sums(held, up_in, up_send, up_recv, target, cut, above)

    def downward(target, cut):
        return sums(held, down_in, down_send, down_recv, target, cut, below)

    def add(target, cut, arriving):
        size = rank // REDUCE_CUTS
        rows = pl.ds(cut * size, size)
        held[target, rows] = held[target, rows] + arriving[target, rows]

    for target in targets:
        part_a, part_b = piece(target, other_x)
        cross_out[target, :, :wa] = part_a
        cross_out[target, :, wa:] = part_b
        for cut in range(REDUCE_CUTS):
            over(target, cut).start()
    for target in targets:
        part_a, part_b = piece(target, x)
        held[target, :, :wa] = part_a
        held[target, :, wa:] = part_b

    for target in targets[:-1]:
        for cut in range(REDUCE_CUTS):
            over(target, cut).wait_recv()
            add(target, cut, cross_in)

            @pl.when(z < target)
            def _():
                @pl.when(has_below)
                def _():
                    upward(target, cut).wait_recv()
                    add(target, cut, up_in)

                upward(target, cut).start()

            @pl.when(z > target)
            def _():
                @pl.when(has_above)
                def _():
                    downward(target, cut).wait_recv()
                    add(target, cut, down_in)

                downward(target, cut).start()

    load_na.wait()
    load_nb.wait()
    scale = noise_ratio * clip_bound
    for cut in range(REDUCE_CUTS):
        over(z, cut).wait_recv()
        add(z, cut, cross_in)

        @pl.when(has_below)
        def _():
            upward(z, cut).wait_recv()
            add(z, cut, up_in)

        @pl.when(has_above)
        def _():
            downward(z, cut).wait_recv()
            add(z, cut, down_in)

    out_a_ref[0] = (held[z, :, :wa] + scale * noise_a[...]) / examples
    out_b_ref[0] = (held[z, :, wa:] + scale * noise_b[...]) / examples

    for row in [z] + rows_of:
        for part in parts:
            pass_on(part, row, finish)
    for target in targets:
        for cut in range(REDUCE_CUTS):
            over(target, cut).wait_send()

            @pl.when(z < target)
            def _():
                upward(target, cut).wait_send()

            @pl.when(z > target)
            def _():
                downward(target, cut).wait_send()


def fused(depth, inputs, rows, down, up, noise_a, noise_b):
    rank, wa = down.shape[1:]
    wb = up.shape[2]
    dp = depth * INNER
    f32, bf16 = jnp.float32, jnp.bfloat16
    dma = pltpu.SemaphoreType.DMA
    return pl.pallas_call(
        functools.partial(kernel, depth),
        out_shape=(
            pltpu.VMEM(noise_a.shape, f32),
            pltpu.VMEM(noise_b.shape, f32),
        ),
        in_specs=[pl.BlockSpec(memory_space=pltpu.HBM)] * 6,
        out_specs=(pl.BlockSpec(memory_space=pltpu.VMEM), pl.BlockSpec(memory_space=pltpu.VMEM)),
        scratch_shapes=[
            pltpu.VMEM(inputs.shape, bf16),
            pltpu.VMEM(rows.shape, bf16),
            pltpu.VMEM((dp, rank, wa), bf16),
            pltpu.VMEM((dp, rank, wb), bf16),
            pltpu.VMEM((rank, wa), f32),
            pltpu.VMEM((rank, wb), f32),
            pltpu.VMEM((2, rank, SEQ), f32),
            pltpu.VMEM((2, rank, SEQ), f32),
            pltpu.VMEM((8, 128), f32),
            pltpu.VMEM((8, 128), f32),
            pltpu.VMEM((depth, rank, wa + wb), f32),
            pltpu.VMEM((depth, rank, wa + wb), f32),
            pltpu.VMEM((depth, rank, wa + wb), f32),
            pltpu.VMEM((depth, rank, wa + wb), f32),
            pltpu.VMEM((depth, rank, wa + wb), f32),
            dma((6,)),
            dma((3, 2, GATHER_CUTS, depth)),
            dma((2, GATHER_CUTS, dp)),
            dma((2,)),
            dma((2,)),
            dma((depth, REDUCE_CUTS)),
            dma((depth, REDUCE_CUTS)),
            dma((depth, REDUCE_CUTS)),
            dma((depth, REDUCE_CUTS)),
            dma((depth, REDUCE_CUTS)),
            dma((depth, REDUCE_CUTS)),
        ],
        compiler_params=pltpu.CompilerParams(
            collective_id=0, has_side_effects=True, vmem_limit_bytes=56 * 1024 * 1024
        ),
        cost_estimate=pl.CostEstimate(
            flops=6 * rank * SEQ * dp * (wa + wb),
            bytes_accessed=2 * SEQ * dp * (wa + wb),
            transcendentals=0,
        ),
    )(inputs, rows, down, up, noise_a, noise_b)


def solution(mesh):
    in_specs = (
        P(("groups", "dp"), "mp"),
        P(("groups", "dp"), "mp"),
        P("mp", None, "dp"),
        P("mp", None, "dp"),
        P("mp", "groups", "dp"),
        P("mp", "groups", "dp"),
    )
    out_specs = (P("mp", "groups", "dp"), P("mp", "groups", "dp"))
    devices = mesh.shape["dp"]

    def body(inputs, rows, down, up, noise_a, noise_b):
        fits = (
            devices % INNER == 0
            and 4 <= devices <= 16
            and mesh.shape["mp"] == 2
            and inputs.shape[0] == SEQ
            and down.shape[2] % 128 == 0
            and up.shape[2] % 128 == 0
        )
        if fits:
            return fused(devices // INNER, inputs, rows, down, up, noise_a, noise_b)
        return per_device(inputs, rows, down, up, noise_a, noise_b)

    return jax.shard_map(
        body, mesh=mesh, in_specs=in_specs, out_specs=out_specs, check_vma=False
    )
```

```python
import functools
import math

import jax
import jax.numpy as jnp
from jax import lax
from jax.experimental import pallas as pl
from jax.experimental.pallas import tpu as pltpu
from jax.sharding import PartitionSpec as P

MODEL_WIDTH = 4096
UP_HIDDEN_UNITS = 14336
ADAPTER_RANK = 64
SEQ = 256

INNER = 2
GATHER_CUTS = 2
REDUCE_CUTS = 2

clip_ratio = 4.0
noise_ratio = 0.005
clip_bound = clip_ratio * math.sqrt(SEQ * ADAPTER_RANK * (MODEL_WIDTH + UP_HIDDEN_UNITS))


def contract_last(left, right):
    return lax.dot_general(
        left, right, (((1,), (1,)), ((), ())), preferred_element_type=jnp.float32
    )


def contract_first(left, right):
    return lax.dot_general(
        left, right, (((0,), (0,)), ((), ())), preferred_element_type=jnp.float32
    )


def per_device(
    inputs,
    output_gradient_rows,
    down_adapter_weight,
    up_adapter_weight,
    down_gradient_noise,
    up_gradient_noise,
):
    a_half, b_half = (
        lax.all_gather(down_adapter_weight, "dp", axis=2, tiled=True),
        lax.all_gather(up_adapter_weight, "dp", axis=2, tiled=True),
    )
    u_part = contract_last(inputs, a_half[0])
    v_part = contract_last(output_gradient_rows, b_half[0])
    u_proj, v_proj = lax.psum((u_part, v_part), "mp")
    u_low = u_proj.astype(jnp.bfloat16)
    v_low = v_proj.astype(jnp.bfloat16)
    count = inputs.shape[0] // SEQ
    x_rows = inputs.reshape(count, SEQ, inputs.shape[1])
    g_rows = output_gradient_rows.reshape(count, SEQ, output_gradient_rows.shape[1])
    u_rows = u_low.reshape(count, SEQ, ADAPTER_RANK)
    v_rows = v_low.reshape(count, SEQ, ADAPTER_RANK)
    grad_x = jnp.einsum("esr,esd->erd", v_rows, x_rows, preferred_element_type=jnp.float32)
    grad_g = jnp.einsum("esr,esf->erf", u_rows, g_rows, preferred_element_type=jnp.float32)
    local_sq = jnp.sum(grad_x * grad_x, axis=(1, 2)) + jnp.sum(grad_g * grad_g, axis=(1, 2))
    squares = lax.psum(local_sq, "mp")
    clip_rate = clip_bound / jnp.maximum(jnp.sqrt(squares), clip_bound)
    token_rate = jnp.repeat(clip_rate, SEQ)
    scaled_u = (u_proj * token_rate[:, None]).astype(jnp.bfloat16)
    scaled_v = (v_proj * token_rate[:, None]).astype(jnp.bfloat16)
    part_a = contract_first(scaled_v, inputs)[None]
    part_b = contract_first(scaled_u, output_gradient_rows)[None]
    total_a, total_b = (
        lax.psum_scatter(part_a, "dp", scatter_dimension=2, tiled=True),
        lax.psum_scatter(part_b, "dp", scatter_dimension=2, tiled=True),
    )
    examples = count * lax.axis_size("dp")
    grad_a = (total_a + noise_ratio * clip_bound * down_gradient_noise) / examples
    grad_b = (total_b + noise_ratio * clip_bound * up_gradient_noise) / examples
    return (grad_a, grad_b)


def remote(src, dst, send_sem, recv_sem, axis, index):
    return pltpu.make_async_remote_copy(
        src_ref=src,
        dst_ref=dst,
        send_sem=send_sem,
        recv_sem=recv_sem,
        device_id={axis: index},
        device_id_type=pl.DeviceIdType.MESH,
    )


def gather_order(depth):
    return [sorted((p for p in range(depth) if p != z), key=lambda p: abs(p - z)) for z in range(depth)]


def reduce_order(depth):
    table = []
    for z in range(depth):
        up = list(range(depth - 1, z, -1))
        down = list(range(z))
        table.append((up + down if len(up) >= len(down) else down + up) + [z])
    return table


def pick(table, step, z):
    entry = jnp.int32(table[0][step])
    for row in range(1, len(table)):
        entry = jnp.where(z == row, jnp.int32(table[row][step]), entry)
    return entry


def kernel(
    depth,
    x_ref, g_ref, a_ref, b_ref, noise_a_ref, noise_b_ref,
    out_a_ref, out_b_ref,
    x_rows, g_rows, a_all, b_all, noise_a, noise_b,
    uv_mine, uv_other, sq_mine, sq_other,
    cross_out, cross_in, held, up_in, down_in,
    local_sem, gather_send, gather_recv, pair_send, pair_recv,
    cross_send, cross_recv, up_send, up_recv, down_send, down_recv,
):
    dp = lax.axis_index("dp")
    mp = lax.axis_index("mp")
    z = dp // INNER
    x = dp % INNER
    other_x = 1 - x
    across = z * INNER + other_x
    above = dp + INNER
    below = dp - INNER
    rank = a_ref.shape[1]
    wa = a_ref.shape[2]
    wb = b_ref.shape[2]
    examples = depth * INNER
    has_above = z < depth - 1
    has_below = z > 0

    def local(src, dst, index):
        copy = pltpu.make_async_copy(src, dst, local_sem.at[index])
        copy.start()
        return copy

    own_a = local(a_ref.at[0], a_all.at[dp], 0)
    own_b = local(b_ref.at[0], b_all.at[dp], 1)
    load_x = local(x_ref, x_rows, 2)
    load_g = local(g_ref, g_rows, 3)
    load_na = local(noise_a_ref.at[0], noise_a, 4)
    load_nb = local(noise_b_ref.at[0], noise_b, 5)

    barrier = pltpu.get_barrier_semaphore()

    def greet(axis, index):
        pl.semaphore_signal(
            barrier, inc=1, device_id={axis: index}, device_id_type=pl.DeviceIdType.MESH
        )

    greet("dp", across)
    greet("mp", 1 - mp)

    @pl.when(has_above)
    def _():
        greet("dp", above)

    @pl.when(has_below)
    def _():
        greet("dp", below)

    @pl.when(has_above & has_below)
    def _():
        pl.semaphore_wait(barrier, 4)

    @pl.when(jnp.logical_not(has_above & has_below))
    def _():
        pl.semaphore_wait(barrier, 3)

    own_a.wait()
    own_b.wait()

    def chunk(which, cut):
        size = rank // GATHER_CUTS
        return ((a_all, b_all)[which]), pl.ds(cut * size, size)

    parts = [(which, cut) for cut in range(GATHER_CUTS) for which in (0, 1)]

    def give(part, row, way, index):
        which, cut = part
        whole, rows = chunk(which, cut)
        slot = row * INNER + x
        return remote(
            whole.at[slot, rows], whole.at[slot, rows],
            gather_send.at[way, which, cut, row], gather_recv.at[which, cut, slot],
            "dp", index,
        )

    def take(part, slot):
        which, cut = part
        whole, rows = chunk(which, cut)
        remote(
            whole.at[slot, rows], whole.at[slot, rows],
            gather_send.at[0, which, cut, 0], gather_recv.at[which, cut, slot],
            "dp", across,
        ).wait_recv()

    def pass_on(part, row, act):
        @pl.when(has_above & (row <= z))
        def _():
            act(give(part, row, 1, above))

        @pl.when(has_below & (row >= z))
        def _():
            act(give(part, row, 2, below))

        act(give(part, row, 0, across))

    def start(copy):
        copy.start()

    def finish(copy):
        copy.wait_send()

    def project(slot):
        u = contract_last(a_all[slot], x_rows[:, pl.ds(pl.multiple_of(slot * wa, 128), wa)])
        v = contract_last(b_all[slot], g_rows[:, pl.ds(pl.multiple_of(slot * wb, 128), wb)])
        return u, v

    for part in parts:
        pass_on(part, z, start)
    near = gather_order(depth)
    rows_of = [pick(near, step, z) for step in range(depth - 1)]
    load_x.wait()
    load_g.wait()
    u, v = project(dp)

    def take_across(row, u, v):
        slot = row * INNER + other_x
        for part in parts:
            take(part, slot)
        more = project(slot)
        return u + more[0], v + more[1]

    for row in rows_of:
        for part in parts:
            take(part, row * INNER + x)
            pass_on(part, row, start)
    for row in rows_of:
        more = project(row * INNER + x)
        u, v = u + more[0], v + more[1]
    for row in [z] + rows_of:
        u, v = take_across(row, u, v)

    uv_mine[0] = u
    uv_mine[1] = v
    copy = remote(uv_mine, uv_other, pair_send.at[0], pair_recv.at[0], "mp", 1 - mp)
    copy.start()
    copy.wait()
    u = u + uv_other[0]
    v = v + uv_other[1]
    u_low = u.astype(jnp.bfloat16)
    v_low = v.astype(jnp.bfloat16)

    def product(low, rows, block, width):
        return jnp.dot(
            low, rows[:, block * width:(block + 1) * width], preferred_element_type=jnp.float32
        )

    sq_a = jnp.zeros((1, wa), jnp.float32)
    sq_b = jnp.zeros((1, wb), jnp.float32)
    for block in range(examples):
        part = product(v_low, x_rows, block, wa)
        sq_a = sq_a + jnp.sum(part * part, axis=0, keepdims=True)
        part = product(u_low, g_rows, block, wb)
        sq_b = sq_b + jnp.sum(part * part, axis=0, keepdims=True)
    sq = jnp.sum(sq_a, axis=1, keepdims=True) + jnp.sum(sq_b, axis=1, keepdims=True)
    sq_mine[...] = jnp.broadcast_to(sq, sq_mine.shape)
    copy = remote(sq_mine, sq_other, pair_send.at[1], pair_recv.at[1], "mp", 1 - mp)
    copy.start()
    copy.wait()
    squares = sq_mine[...] + sq_other[...]
    rate = (clip_bound / jnp.maximum(jnp.sqrt(squares), clip_bound))[0:1, 0:1]
    u_scaled = (u * rate).astype(jnp.bfloat16)
    v_scaled = (v * rate).astype(jnp.bfloat16)

    def piece(target, side):
        slot = target * INNER + side
        part_a = jnp.dot(
            v_scaled, x_rows[:, pl.ds(pl.multiple_of(slot * wa, 128), wa)],
            preferred_element_type=jnp.float32,
        )
        part_b = jnp.dot(
            u_scaled, g_rows[:, pl.ds(pl.multiple_of(slot * wb, 128), wb)],
            preferred_element_type=jnp.float32,
        )
        return part_a, part_b

    far = reduce_order(depth)
    targets = [pick(far, step, z) for step in range(depth)]

    def sums(src, dst, send_sem, recv_sem, target, cut, index):
        size = rank // REDUCE_CUTS
        rows = pl.ds(cut * size, size)
        return remote(
            src.at[target, rows], dst.at[target, rows],
            send_sem.at[target, cut], recv_sem.at[target, cut], "dp", index,
        )

    def over(target, cut):
        return sums(cross_out, cross_in, cross_send, cross_recv, target, cut, across)

    def upward(target, cut):
        return sums(held, up_in, up_send, up_recv, target, cut, above)

    def downward(target, cut):
        return sums(held, down_in, down_send, down_recv, target, cut, below)

    def add(target, cut, arriving):
        size = rank // REDUCE_CUTS
        rows = pl.ds(cut * size, size)
        held[target, rows] = held[target, rows] + arriving[target, rows]

    for target in targets:
        part_a, part_b = piece(target, other_x)
        cross_out[target, :, :wa] = part_a
        cross_out[target, :, wa:] = part_b
        for cut in range(REDUCE_CUTS):
            over(target, cut).start()
    for target in targets:
        part_a, part_b = piece(target, x)
        held[target, :, :wa] = part_a
        held[target, :, wa:] = part_b

    for target in targets[:-1]:
        for cut in range(REDUCE_CUTS):
            over(target, cut).wait_recv()
            add(target, cut, cross_in)

            @pl.when(z < target)
            def _():
                @pl.when(has_below)
                def _():
                    upward(target, cut).wait_recv()
                    add(target, cut, up_in)

                upward(target, cut).start()

            @pl.when(z > target)
            def _():
                @pl.when(has_above)
                def _():
                    downward(target, cut).wait_recv()
                    add(target, cut, down_in)

                downward(target, cut).start()

    load_na.wait()
    load_nb.wait()
    scale = noise_ratio * clip_bound
    for cut in range(REDUCE_CUTS):
        over(z, cut).wait_recv()
        add(z, cut, cross_in)

        @pl.when(has_below)
        def _():
            upward(z, cut).wait_recv()
            add(z, cut, up_in)

        @pl.when(has_above)
        def _():
            downward(z, cut).wait_recv()
            add(z, cut, down_in)

    out_a_ref[0] = (held[z, :, :wa] + scale * noise_a[...]) / examples
    out_b_ref[0] = (held[z, :, wa:] + scale * noise_b[...]) / examples

    for row in [z] + rows_of:
        for part in parts:
            pass_on(part, row, finish)
    for target in targets:
        for cut in range(REDUCE_CUTS):
            over(target, cut).wait_send()

            @pl.when(z < target)
            def _():
                upward(target, cut).wait_send()

            @pl.when(z > target)
            def _():
                downward(target, cut).wait_send()


def fused(depth, inputs, rows, down, up, noise_a, noise_b):
    rank, wa = down.shape[1:]
    wb = up.shape[2]
    dp = depth * INNER
    f32, bf16 = jnp.float32, jnp.bfloat16
    dma = pltpu.SemaphoreType.DMA
    return pl.pallas_call(
        functools.partial(kernel, depth),
        out_shape=(
            pltpu.VMEM(noise_a.shape, f32),
            pltpu.VMEM(noise_b.shape, f32),
        ),
        in_specs=[pl.BlockSpec(memory_space=pltpu.HBM)] * 6,
        out_specs=(pl.BlockSpec(memory_space=pltpu.VMEM), pl.BlockSpec(memory_space=pltpu.VMEM)),
        scratch_shapes=[
            pltpu.VMEM(inputs.shape, bf16),
            pltpu.VMEM(rows.shape, bf16),
            pltpu.VMEM((dp, rank, wa), bf16),
            pltpu.VMEM((dp, rank, wb), bf16),
            pltpu.VMEM((rank, wa), f32),
            pltpu.VMEM((rank, wb), f32),
            pltpu.VMEM((2, rank, SEQ), f32),
            pltpu.VMEM((2, rank, SEQ), f32),
            pltpu.VMEM((8, 128), f32),
            pltpu.VMEM((8, 128), f32),
            pltpu.VMEM((depth, rank, wa + wb), f32),
            pltpu.VMEM((depth, rank, wa + wb), f32),
            pltpu.VMEM((depth, rank, wa + wb), f32),
            pltpu.VMEM((depth, rank, wa + wb), f32),
            pltpu.VMEM((depth, rank, wa + wb), f32),
            dma((6,)),
            dma((3, 2, GATHER_CUTS, depth)),
            dma((2, GATHER_CUTS, dp)),
            dma((2,)),
            dma((2,)),
            dma((depth, REDUCE_CUTS)),
            dma((depth, REDUCE_CUTS)),
            dma((depth, REDUCE_CUTS)),
            dma((depth, REDUCE_CUTS)),
            dma((depth, REDUCE_CUTS)),
            dma((depth, REDUCE_CUTS)),
        ],
        compiler_params=pltpu.CompilerParams(
            collective_id=0, has_side_effects=True, vmem_limit_bytes=56 * 1024 * 1024
        ),
        cost_estimate=pl.CostEstimate(
            flops=6 * rank * SEQ * dp * (wa + wb),
            bytes_accessed=2 * SEQ * dp * (wa + wb),
            transcendentals=0,
        ),
    )(inputs, rows, down, up, noise_a, noise_b)


def solution(mesh):
    in_specs = (
        P(("groups", "dp"), "mp"),
        P(("groups", "dp"), "mp"),
        P("mp", None, "dp"),
        P("mp", None, "dp"),
        P("mp", "groups", "dp"),
        P("mp", "groups", "dp"),
    )
    out_specs = (P("mp", "groups", "dp"), P("mp", "groups", "dp"))
    devices = mesh.shape["dp"]

    def body(inputs, rows, down, up, noise_a, noise_b):
        fits = (
            devices % INNER == 0
            and 4 <= devices <= 16
            and mesh.shape["mp"] == 2
            and inputs.shape[0] == SEQ
            and down.shape[2] % 128 == 0
            and up.shape[2] % 128 == 0
        )
        if fits:
            return fused(devices // INNER, inputs, rows, down, up, noise_a, noise_b)
        return per_device(inputs, rows, down, up, noise_a, noise_b)

    return jax.shard_map(
        body, mesh=mesh, in_specs=in_specs, out_specs=out_specs, check_vma=False
    )
```

```python
import functools
import math

import jax
import jax.numpy as jnp
from jax import lax
from jax.experimental import pallas as pl
from jax.experimental.pallas import tpu as pltpu
from jax.sharding import PartitionSpec as P

MODEL_WIDTH = 4096
UP_HIDDEN_UNITS = 14336
ADAPTER_RANK = 64
SEQ = 256

INNER = 2
GATHER_CUTS = 2
REDUCE_CUTS = 2

clip_ratio = 4.0
noise_ratio = 0.005
clip_bound = clip_ratio * math.sqrt(SEQ * ADAPTER_RANK * (MODEL_WIDTH + UP_HIDDEN_UNITS))


def contract_last(left, right):
    return lax.dot_general(
        left, right, (((1,), (1,)), ((), ())), preferred_element_type=jnp.float32
    )


def contract_first(left, right):
    return lax.dot_general(
        left, right, (((0,), (0,)), ((), ())), preferred_element_type=jnp.float32
    )


def per_device(
    inputs,
    output_gradient_rows,
    down_adapter_weight,
    up_adapter_weight,
    down_gradient_noise,
    up_gradient_noise,
):
    a_half, b_half = (
        lax.all_gather(down_adapter_weight, "dp", axis=2, tiled=True),
        lax.all_gather(up_adapter_weight, "dp", axis=2, tiled=True),
    )
    u_part = contract_last(inputs, a_half[0])
    v_part = contract_last(output_gradient_rows, b_half[0])
    u_proj, v_proj = lax.psum((u_part, v_part), "mp")
    u_low = u_proj.astype(jnp.bfloat16)
    v_low = v_proj.astype(jnp.bfloat16)
    count = inputs.shape[0] // SEQ
    x_rows = inputs.reshape(count, SEQ, inputs.shape[1])
    g_rows = output_gradient_rows.reshape(count, SEQ, output_gradient_rows.shape[1])
    u_rows = u_low.reshape(count, SEQ, ADAPTER_RANK)
    v_rows = v_low.reshape(count, SEQ, ADAPTER_RANK)
    grad_x = jnp.einsum("esr,esd->erd", v_rows, x_rows, preferred_element_type=jnp.float32)
    grad_g = jnp.einsum("esr,esf->erf", u_rows, g_rows, preferred_element_type=jnp.float32)
    local_sq = jnp.sum(grad_x * grad_x, axis=(1, 2)) + jnp.sum(grad_g * grad_g, axis=(1, 2))
    squares = lax.psum(local_sq, "mp")
    clip_rate = clip_bound / jnp.maximum(jnp.sqrt(squares), clip_bound)
    token_rate = jnp.repeat(clip_rate, SEQ)
    scaled_u = (u_proj * token_rate[:, None]).astype(jnp.bfloat16)
    scaled_v = (v_proj * token_rate[:, None]).astype(jnp.bfloat16)
    part_a = contract_first(scaled_v, inputs)[None]
    part_b = contract_first(scaled_u, output_gradient_rows)[None]
    total_a, total_b = (
        lax.psum_scatter(part_a, "dp", scatter_dimension=2, tiled=True),
        lax.psum_scatter(part_b, "dp", scatter_dimension=2, tiled=True),
    )
    examples = count * lax.axis_size("dp")
    grad_a = (total_a + noise_ratio * clip_bound * down_gradient_noise) / examples
    grad_b = (total_b + noise_ratio * clip_bound * up_gradient_noise) / examples
    return (grad_a, grad_b)


def remote(src, dst, send_sem, recv_sem, axis, index):
    return pltpu.make_async_remote_copy(
        src_ref=src,
        dst_ref=dst,
        send_sem=send_sem,
        recv_sem=recv_sem,
        device_id={axis: index},
        device_id_type=pl.DeviceIdType.MESH,
    )


def gather_order(depth):
    return [sorted((p for p in range(depth) if p != z), key=lambda p: abs(p - z)) for z in range(depth)]


def reduce_order(depth):
    table = []
    for z in range(depth):
        up = list(range(depth - 1, z, -1))
        down = list(range(z))
        table.append((up + down if len(up) >= len(down) else down + up) + [z])
    return table


def pick(table, step, z):
    entry = jnp.int32(table[0][step])
    for row in range(1, len(table)):
        entry = jnp.where(z == row, jnp.int32(table[row][step]), entry)
    return entry


def kernel(
    depth,
    x_ref, g_ref, a_ref, b_ref, noise_a_ref, noise_b_ref,
    out_a_ref, out_b_ref,
    x_rows, g_rows, a_all, b_all, noise_a, noise_b,
    uv_mine, uv_other, sq_mine, sq_other,
    cross_out, cross_in, held, up_in, down_in,
    local_sem, gather_send, gather_recv, pair_send, pair_recv,
    cross_send, cross_recv, up_send, up_recv, down_send, down_recv,
):
    dp = lax.axis_index("dp")
    mp = lax.axis_index("mp")
    z = dp // INNER
    x = dp % INNER
    other_x = 1 - x
    across = z * INNER + other_x
    above = dp + INNER
    below = dp - INNER
    rank = a_ref.shape[1]
    wa = a_ref.shape[2]
    wb = b_ref.shape[2]
    examples = depth * INNER
    has_above = z < depth - 1
    has_below = z > 0

    def local(src, dst, index):
        copy = pltpu.make_async_copy(src, dst, local_sem.at[index])
        copy.start()
        return copy

    own_a = local(a_ref.at[0], a_all.at[dp], 0)
    own_b = local(b_ref.at[0], b_all.at[dp], 1)
    load_x = local(x_ref, x_rows, 2)
    load_g = local(g_ref, g_rows, 3)
    load_na = local(noise_a_ref.at[0], noise_a, 4)
    load_nb = local(noise_b_ref.at[0], noise_b, 5)

    barrier = pltpu.get_barrier_semaphore()

    def greet(axis, index):
        pl.semaphore_signal(
            barrier, inc=1, device_id={axis: index}, device_id_type=pl.DeviceIdType.MESH
        )

    greet("dp", across)
    greet("mp", 1 - mp)

    @pl.when(has_above)
    def _():
        greet("dp", above)

    @pl.when(has_below)
    def _():
        greet("dp", below)

    @pl.when(has_above & has_below)
    def _():
        pl.semaphore_wait(barrier, 4)

    @pl.when(jnp.logical_not(has_above & has_below))
    def _():
        pl.semaphore_wait(barrier, 3)

    own_a.wait()
    own_b.wait()

    def chunk(which, cut):
        size = rank // GATHER_CUTS
        return ((a_all, b_all)[which]), pl.ds(cut * size, size)

    parts = [(which, cut) for cut in range(GATHER_CUTS) for which in (0, 1)]

    def give(part, row, way, index):
        which, cut = part
        whole, rows = chunk(which, cut)
        slot = row * INNER + x
        return remote(
            whole.at[slot, rows], whole.at[slot, rows],
            gather_send.at[way, which, cut, row], gather_recv.at[which, cut, slot],
            "dp", index,
        )

    def take(part, slot):
        which, cut = part
        whole, rows = chunk(which, cut)
        remote(
            whole.at[slot, rows], whole.at[slot, rows],
            gather_send.at[0, which, cut, 0], gather_recv.at[which, cut, slot],
            "dp", across,
        ).wait_recv()

    def pass_on(part, row, act):
        @pl.when(has_above & (row <= z))
        def _():
            act(give(part, row, 1, above))

        @pl.when(has_below & (row >= z))
        def _():
            act(give(part, row, 2, below))

        act(give(part, row, 0, across))

    def start(copy):
        copy.start()

    def finish(copy):
        copy.wait_send()

    def project(slot):
        u = contract_last(a_all[slot], x_rows[:, pl.ds(pl.multiple_of(slot * wa, 128), wa)])
        v = contract_last(b_all[slot], g_rows[:, pl.ds(pl.multiple_of(slot * wb, 128), wb)])
        return u, v

    for part in parts:
        pass_on(part, z, start)
    near = gather_order(depth)
    rows_of = [pick(near, step, z) for step in range(depth - 1)]

    def take_across(row, u, v):
        slot = row * INNER + other_x
        for part in parts:
            take(part, slot)
        more = project(slot)
        return u + more[0], v + more[1]

    for row in rows_of:
        for part in parts:
            take(part, row * INNER + x)
            pass_on(part, row, start)
    load_x.wait()
    load_g.wait()
    u, v = project(dp)
    for row in rows_of:
        more = project(row * INNER + x)
        u, v = u + more[0], v + more[1]
    for row in [z] + rows_of:
        u, v = take_across(row, u, v)

    uv_mine[0] = u
    uv_mine[1] = v
    copy = remote(uv_mine, uv_other, pair_send.at[0], pair_recv.at[0], "mp", 1 - mp)
    copy.start()
    copy.wait()
    u = u + uv_other[0]
    v = v + uv_other[1]
    u_low = u.astype(jnp.bfloat16)
    v_low = v.astype(jnp.bfloat16)

    def product(low, rows, block, width):
        return jnp.dot(
            low, rows[:, block * width:(block + 1) * width], preferred_element_type=jnp.float32
        )

    sq_a = jnp.zeros((1, wa), jnp.float32)
    sq_b = jnp.zeros((1, wb), jnp.float32)
    for block in range(examples):
        part = product(v_low, x_rows, block, wa)
        sq_a = sq_a + jnp.sum(part * part, axis=0, keepdims=True)
        part = product(u_low, g_rows, block, wb)
        sq_b = sq_b + jnp.sum(part * part, axis=0, keepdims=True)
    sq = jnp.sum(sq_a, axis=1, keepdims=True) + jnp.sum(sq_b, axis=1, keepdims=True)
    sq_mine[...] = jnp.broadcast_to(sq, sq_mine.shape)
    copy = remote(sq_mine, sq_other, pair_send.at[1], pair_recv.at[1], "mp", 1 - mp)
    copy.start()
    copy.wait()
    squares = sq_mine[...] + sq_other[...]
    rate = (clip_bound / jnp.maximum(jnp.sqrt(squares), clip_bound))[0:1, 0:1]
    u_scaled = (u * rate).astype(jnp.bfloat16)
    v_scaled = (v * rate).astype(jnp.bfloat16)

    def piece(target, side):
        slot = target * INNER + side
        part_a = jnp.dot(
            v_scaled, x_rows[:, pl.ds(pl.multiple_of(slot * wa, 128), wa)],
            preferred_element_type=jnp.float32,
        )
        part_b = jnp.dot(
            u_scaled, g_rows[:, pl.ds(pl.multiple_of(slot * wb, 128), wb)],
            preferred_element_type=jnp.float32,
        )
        return part_a, part_b

    far = reduce_order(depth)
    targets = [pick(far, step, z) for step in range(depth)]

    def sums(src, dst, send_sem, recv_sem, target, cut, index):
        size = rank // REDUCE_CUTS
        rows = pl.ds(cut * size, size)
        return remote(
            src.at[target, rows], dst.at[target, rows],
            send_sem.at[target, cut], recv_sem.at[target, cut], "dp", index,
        )

    def over(target, cut):
        return sums(cross_out, cross_in, cross_send, cross_recv, target, cut, across)

    def upward(target, cut):
        return sums(held, up_in, up_send, up_recv, target, cut, above)

    def downward(target, cut):
        return sums(held, down_in, down_send, down_recv, target, cut, below)

    def add(target, cut, arriving):
        size = rank // REDUCE_CUTS
        rows = pl.ds(cut * size, size)
        held[target, rows] = held[target, rows] + arriving[target, rows]

    for target in targets:
        part_a, part_b = piece(target, other_x)
        cross_out[target, :, :wa] = part_a
        cross_out[target, :, wa:] = part_b
        for cut in range(REDUCE_CUTS):
            over(target, cut).start()
    for target in targets:
        part_a, part_b = piece(target, x)
        held[target, :, :wa] = part_a
        held[target, :, wa:] = part_b

    for target in targets[:-1]:
        for cut in range(REDUCE_CUTS):
            over(target, cut).wait_recv()
            add(target, cut, cross_in)

            @pl.when(z < target)
            def _():
                @pl.when(has_below)
                def _():
                    upward(target, cut).wait_recv()
                    add(target, cut, up_in)

                upward(target, cut).start()

            @pl.when(z > target)
            def _():
                @pl.when(has_above)
                def _():
                    downward(target, cut).wait_recv()
                    add(target, cut, down_in)

                downward(target, cut).start()

    load_na.wait()
    load_nb.wait()
    scale = noise_ratio * clip_bound
    for cut in range(REDUCE_CUTS):
        over(z, cut).wait_recv()
        add(z, cut, cross_in)

        @pl.when(has_below)
        def _():
            upward(z, cut).wait_recv()
            add(z, cut, up_in)

        @pl.when(has_above)
        def _():
            downward(z, cut).wait_recv()
            add(z, cut, down_in)

    out_a_ref[0] = (held[z, :, :wa] + scale * noise_a[...]) / examples
    out_b_ref[0] = (held[z, :, wa:] + scale * noise_b[...]) / examples

    for row in [z] + rows_of:
        for part in parts:
            pass_on(part, row, finish)
    for target in targets:
        for cut in range(REDUCE_CUTS):
            over(target, cut).wait_send()

            @pl.when(z < target)
            def _():
                upward(target, cut).wait_send()

            @pl.when(z > target)
            def _():
                downward(target, cut).wait_send()


def fused(depth, inputs, rows, down, up, noise_a, noise_b):
    rank, wa = down.shape[1:]
    wb = up.shape[2]
    dp = depth * INNER
    f32, bf16 = jnp.float32, jnp.bfloat16
    dma = pltpu.SemaphoreType.DMA
    return pl.pallas_call(
        functools.partial(kernel, depth),
        out_shape=(
            pltpu.VMEM(noise_a.shape, f32),
            pltpu.VMEM(noise_b.shape, f32),
        ),
        in_specs=[pl.BlockSpec(memory_space=pltpu.HBM)] * 6,
        out_specs=(pl.BlockSpec(memory_space=pltpu.VMEM), pl.BlockSpec(memory_space=pltpu.VMEM)),
        scratch_shapes=[
            pltpu.VMEM(inputs.shape, bf16),
            pltpu.VMEM(rows.shape, bf16),
            pltpu.VMEM((dp, rank, wa), bf16),
            pltpu.VMEM((dp, rank, wb), bf16),
            pltpu.VMEM((rank, wa), f32),
            pltpu.VMEM((rank, wb), f32),
            pltpu.VMEM((2, rank, SEQ), f32),
            pltpu.VMEM((2, rank, SEQ), f32),
            pltpu.VMEM((8, 128), f32),
            pltpu.VMEM((8, 128), f32),
            pltpu.VMEM((depth, rank, wa + wb), f32),
            pltpu.VMEM((depth, rank, wa + wb), f32),
            pltpu.VMEM((depth, rank, wa + wb), f32),
            pltpu.VMEM((depth, rank, wa + wb), f32),
            pltpu.VMEM((depth, rank, wa + wb), f32),
            dma((6,)),
            dma((3, 2, GATHER_CUTS, depth)),
            dma((2, GATHER_CUTS, dp)),
            dma((2,)),
            dma((2,)),
            dma((depth, REDUCE_CUTS)),
            dma((depth, REDUCE_CUTS)),
            dma((depth, REDUCE_CUTS)),
            dma((depth, REDUCE_CUTS)),
            dma((depth, REDUCE_CUTS)),
            dma((depth, REDUCE_CUTS)),
        ],
        compiler_params=pltpu.CompilerParams(
            collective_id=0, has_side_effects=True, vmem_limit_bytes=56 * 1024 * 1024
        ),
        cost_estimate=pl.CostEstimate(
            flops=6 * rank * SEQ * dp * (wa + wb),
            bytes_accessed=2 * SEQ * dp * (wa + wb),
            transcendentals=0,
        ),
    )(inputs, rows, down, up, noise_a, noise_b)


def solution(mesh):
    in_specs = (
        P(("groups", "dp"), "mp"),
        P(("groups", "dp"), "mp"),
        P("mp", None, "dp"),
        P("mp", None, "dp"),
        P("mp", "groups", "dp"),
        P("mp", "groups", "dp"),
    )
    out_specs = (P("mp", "groups", "dp"), P("mp", "groups", "dp"))
    devices = mesh.shape["dp"]

    def body(inputs, rows, down, up, noise_a, noise_b):
        fits = (
            devices % INNER == 0
            and 4 <= devices <= 16
            and mesh.shape["mp"] == 2
            and inputs.shape[0] == SEQ
            and down.shape[2] % 128 == 0
            and up.shape[2] % 128 == 0
        )
        if fits:
            return fused(devices // INNER, inputs, rows, down, up, noise_a, noise_b)
        return per_device(inputs, rows, down, up, noise_a, noise_b)

    return jax.shard_map(
        body, mesh=mesh, in_specs=in_specs, out_specs=out_specs, check_vma=False
    )
```
